32 devices in a mesh: parts: 2 (over y), blk: 4 (over z), rhs: 2 (over x), sub: 2 (over core).
Axes of the slice: x: 2, y: 2, z: 4, core: 2. Of those that a mesh axis runs over, the one named last changes fastest.
Arguments:
- currents: bfloat16 [2, 80, 24576], P(None, None, ('parts', 'blk', 'rhs')), parts along dimension 2, may hold values from -6 to 6
- tri_cent: float32 [3, 16384], P(None, 'parts'), parts along dimension 1, may hold values from 0 to 10
- edge_tris: int32 [2, 24576], P(None, 'parts'), parts along dimension 1, may hold values from 0 to 8191
- edge_len: float32 [24576], P('parts'), parts along dimension 0, may hold values from 0.5 to 2
- near_col: int32 [384, 4], P(('parts', 'blk', 'sub'), 'rhs'), parts along dimension 0, may hold values from 0 to 191, as said below
- near_val: bfloat16 [384, 4, 64, 128], P(('parts', 'blk', 'sub'), 'rhs'), parts along dimension 0, may hold values from -0.25 to 0.25
- refine_map: int32 [24576], P('parts'), parts along dimension 0, may hold values from 0 to 12287, as said below
- dual_blocks: bfloat16 [384, 64, 128], P(('parts', 'blk', 'sub')), parts along dimension 0, may hold values from -0.5 to 0.5
Outputs:
- calderon: float32 [2, 80, 24576], P(None, 'rhs', ('parts', 'blk', 'sub')), parts along dimension 2
The draws below stay inside these ranges and needn't reach their ends.
There are 2 independent parts, one for each index of `parts`. The reference program is written for one: setup_inputs(seed, part) draws one part's arguments, and reference() takes and returns one part's arrays. A program takes and returns all parts, laid end to end along the dimension named above; each array names one. Nothing has to cross between parts.
Inputs may be any that keep to these rules, and one draw needn't show every extreme that they name: near_col[b, j] lies in (g * 2 + j // 2) * 24 to (g * 2 + j // 2 + 1) * 24 - 1, where g = b // 48. `refine_map`: a permutation; for all s, o below 8, exactly 192 of the entries s * 1536 to (s + 1) * 1536 - 1 lie in o * 1536 to (o + 1) * 1536 - 1.
All inputs are finite; a program needn't handle non-finite values.
Results may differ from the reference program's by a relative error of at most 0.004.
Values may be sent and summed in bfloat16 or wider, within the bound.
A program may use at most 64 MiB of HBM per device.

```python
import math
import jax
import jax.numpy as jnp
from jax import lax

ROWS_DEV = 1536
ANGLES = 80
BS = 64
NEAR_DEV = 2
GROUP = 3072
N = 12288
NTRI = 8192
NRB = 192
NEAR = 4
NBT = 24
OWNERS = 8
N_RHS = 2


def draw_near_col(key, part):
    block_ids = jnp.arange(NRB, dtype=jnp.int32)
    slot_ids = jnp.arange(NEAR, dtype=jnp.int32)
    group_of = block_ids // (GROUP // BS)
    tile_of = slot_ids // NEAR_DEV
    picked = jax.random.randint(key, (NRB, NEAR), 0, NBT, dtype=jnp.int32)
    picked = picked.at[0, 0].set(0).at[NRB - 1, NEAR - 1].set(NBT - 1)
    return ((group_of[:, None] * N_RHS + tile_of[None, :]) * NBT + picked).astype(jnp.int32)


def draw_refine_map(key, part):
    slot_rows = ROWS_DEV // OWNERS
    owner_ids = jnp.arange(OWNERS, dtype=jnp.int32)
    within = jax.vmap(lambda owner_id: jax.random.permutation(jax.random.fold_in(key, owner_id), ROWS_DEV))(owner_ids)
    targets = within.astype(jnp.int32).reshape(OWNERS, OWNERS, slot_rows) + (owner_ids * ROWS_DEV)[:, None, None]
    targets = jnp.transpose(targets, (1, 0, 2)).reshape(OWNERS, ROWS_DEV)
    mixing_key = jax.random.fold_in(key, 104729)
    mixing = jax.vmap(lambda source: jax.random.permutation(jax.random.fold_in(mixing_key, source), ROWS_DEV))(owner_ids)
    return jnp.take_along_axis(targets, mixing.astype(jnp.int32), axis=1).reshape(N).astype(jnp.int32)


def plant(drawn, rng, smallest, largest):
    index_at = [jax.random.randint(jax.random.fold_in(rng, axis), (), 0, length) for axis, length in enumerate(drawn.shape)]
    longest = drawn.shape.index(max(drawn.shape))
    next_to = index_at[:longest] + [(index_at[longest] + 1) % drawn.shape[longest]] + index_at[longest + 1:]
    return drawn.at[tuple(index_at)].set(smallest).at[tuple(next_to)].set(largest)


def block_scale(stream_key, dims, pieces, smallest, top_value):
    level, own = 1.0, jax.random.fold_in(stream_key, 6)
    for position, shards_of in pieces:
        heights = jnp.exp(jax.random.uniform(jax.random.fold_in(own, position), (shards_of,), jnp.float32, smallest / len(pieces), top_value / len(pieces)))
        level = level * jnp.repeat(heights, dims[position] // shards_of).reshape([-1 if axis == position else 1 for axis in range(len(dims))])
    return level


def bell_draw(key, shape, scale, most, pieces=(), kind=jnp.bfloat16):
    loudness = block_scale(key, shape, pieces, -0.22, 0.18) if pieces else 1.0
    drawn = jax.random.normal(key, shape, jnp.float32) * scale * loudness
    return jnp.minimum(jnp.maximum(drawn, -most), most).astype(kind)


def setup_inputs(seed: int = 0, part: int = 0) -> dict:
    key_of = jax.random.split(jax.random.key(seed), 9)
    own_keys = jax.random.split(jax.random.fold_in(key_of[8], part), 9)
    return {
        "currents": bell_draw(own_keys[0], (2, ANGLES, N), 1.0, 6.0, ((2, 8),)),
        "tri_cent": jnp.clip(jax.random.uniform(own_keys[1], (3, NTRI), jnp.float32, 0.0, 10.0), 0.0, 10.0),
        "edge_tris": plant(jax.random.randint(own_keys[2], (2, N), 0, NTRI), jax.random.fold_in(own_keys[2], 1), 0, NTRI - 1).astype(jnp.int32),
        "edge_len": jnp.clip(jnp.exp(jax.random.uniform(own_keys[3], (N,), jnp.float32, math.log(0.5), math.log(2.0))), 0.5, 2.0),
        "near_col": draw_near_col(jax.random.fold_in(jax.random.fold_in(key_of[8], part), 71), part),
        "near_val": bell_draw(own_keys[5], (NRB, NEAR, BS, 2 * BS), (2 * BS * NEAR) ** -0.5, 0.25, ((0, 8), (1, 2))),
        "refine_map": draw_refine_map(jax.random.fold_in(jax.random.fold_in(key_of[8], part), 71), part),
        "dual_blocks": bell_draw(own_keys[7], (NRB, BS, 2 * BS), (2 * BS) ** -0.5, 0.5, ((0, 8),)),
    }


WAVE_NUMBER = 2.0 * math.pi
SOFTENING = 0.1
SPAN_SCALE = 3.0
CHARGE_TERM = 0.5

def geometry(indices, tri_cent, edge_tris, edge_len):
    plus_tri = jnp.take(tri_cent, jnp.take(edge_tris[0], indices), axis=1)
    minus_tri = jnp.take(tri_cent, jnp.take(edge_tris[1], indices), axis=1)
    return (0.5 * (plus_tri + minus_tri), minus_tri - plus_tri, jnp.take(edge_len, indices))

def kernel_tile(columns, rowset, count_all):
    col_pos, col_dir, col_len = columns
    row_pos, row_dir, row_len = rowset
    squared = jnp.zeros((col_pos.shape[1], row_pos.shape[1]), jnp.float32)
    aligned = jnp.zeros((col_pos.shape[1], row_pos.shape[1]), jnp.float32)
    for component in range(3):
        offset = col_pos[component][:, None] - row_pos[component][None, :]
        squared = squared + offset * offset
        aligned = aligned + col_dir[component][:, None] * row_dir[component][None, :]
    distance = jnp.sqrt(squared + SOFTENING * SOFTENING)
    weight = col_len[:, None] * row_len[None, :] * (aligned / (SPAN_SCALE * SPAN_SCALE) - CHARGE_TERM) / (distance * math.sqrt(count_all))
    phases = WAVE_NUMBER * distance
    return jnp.concatenate([(weight * jnp.cos(phases)).astype(jnp.bfloat16), (weight * jnp.sin(phases)).astype(jnp.bfloat16)], 0)

def complex_pairs(real_part, imag_part, where_at):
    return jnp.stack([jnp.stack([real_part, -imag_part], where_at), jnp.stack([imag_part, real_part], where_at)], where_at)

def reference(currents, tri_cent, edge_tris, edge_len, near_col, near_val, refine_map, dual_blocks):
    all_cols = jnp.arange(N, dtype=jnp.int32)
    columns = geometry(all_cols, tri_cent, edge_tris, edge_len)
    stacked = jnp.concatenate([jnp.concatenate([currents[0], -currents[1]], 1), jnp.concatenate([currents[1], currents[0]], 1)], 0)
    row_block = 4 * BS

    def one_block(block_index):
        row_ids = block_index * row_block + jnp.arange(row_block, dtype=jnp.int32)
        tile_pair = kernel_tile(columns, geometry(row_ids, tri_cent, edge_tris, edge_len), N)
        return jnp.dot(stacked, tile_pair, preferred_element_type=jnp.float32)
    far_part = lax.map(one_block, jnp.arange(N // row_block, dtype=jnp.int32))
    far_part = jnp.transpose(far_part, (1, 0, 2)).reshape(2, ANGLES, N)
    col_blocks = currents.reshape(2, ANGLES, NRB, BS)
    chosen = jnp.take(col_blocks, near_col, axis=2).astype(jnp.float32)
    paired = complex_pairs(chosen[0], chosen[1], 0)
    values = near_val.astype(jnp.float32).reshape(NRB, NEAR, BS, 2, BS)
    near_sum = jnp.einsum('bjmtn,otabjn->oabm', values, paired).reshape(2, ANGLES, N)
    coarse_product = (far_part + near_sum).astype(jnp.bfloat16)
    moved = jnp.zeros_like(coarse_product).at[:, :, refine_map].set(coarse_product)
    blocked = moved.astype(jnp.float32).reshape(2, ANGLES, NRB, BS)
    moved_pairs = complex_pairs(blocked[0], blocked[1], 0)
    operator = dual_blocks.astype(jnp.float32).reshape(NRB, BS, 2, BS)
    return jnp.einsum('bmtn,otabn->oabm', operator, moved_pairs).reshape(2, ANGLES, N)
```

```python
import functools
import math

import jax
import jax.numpy as jnp
from jax import lax
from jax.experimental import pallas as pl
from jax.experimental.pallas import tpu as pltpu
from jax.sharding import PartitionSpec as P

ROWS_DEV = 1536
BS = 64
LANES = 128
CENTER = 5.0
SOFT2 = 0.1 * 0.1
SPAN2 = 9.0
CHARGE_TERM = 0.5
COS_C = (0.99995979, -19.73104169, 64.67343113, -82.40355036, 45.64655658)
SIN_C = (6.2830558, -41.33121431, 81.36681529, -74.47800454, 32.78140079)
ROUNDER = 12582912.0

F32 = jnp.float32
BF16 = jnp.bfloat16
NT = (((1,), (1,)), ((), ()))
VMEM_LIMIT = 56 * 1024 * 1024


def split3(x):
    h = x.astype(BF16).astype(F32)
    m = (x - h).astype(BF16).astype(F32)
    return h, m, (x - h - m).astype(BF16).astype(F32)


def lookup(table, ids):
    high = table.shape[0] // 3
    width = ids.shape[1]
    low_id = ids & (LANES - 1)
    high_id = ids >> 7
    lows = lax.broadcasted_iota(jnp.int32, (LANES, width), 0) == low_id
    onehot = jnp.where(lows, 1.0, 0.0).astype(BF16)
    picked = jnp.dot(
        table, jnp.concatenate([onehot] * 3, 0), preferred_element_type=F32
    )
    mask = lax.broadcasted_iota(jnp.int32, (high, width), 0) == high_id
    rows = [
        jnp.sum(jnp.where(mask, picked[c * high : (c + 1) * high], 0.0), axis=0, keepdims=True)
        for c in range(3)
    ]
    return jnp.concatenate(rows + [jnp.zeros((5, width), F32)], 0)


def make_table(tri):
    return jnp.concatenate([piece.astype(BF16) for piece in split3(tri)], 1)


def features(table, ids, lens, count_all, is_rows):
    width = ids.shape[1]
    plus, minus = lookup(table, ids[0:1]), lookup(table, ids[1:2])
    row = lax.broadcasted_iota(jnp.int32, (8, width), 0)
    pos = jnp.where(row < 3, 0.5 * (plus + minus) - CENTER, 0.0)
    norm = jnp.sum(pos * pos, axis=0, keepdims=True)
    ends = (minus - plus) * lens + jnp.where(row == 3, lens, 0.0)
    if is_rows:
        scale = 1.0
    else:
        norm = norm + SOFT2
        scale = jnp.where(row == 3, -CHARGE_TERM, 1.0 / SPAN2) / math.sqrt(count_all)
    ends = ends * scale
    h, m, l = split3(pos)
    nh, nm, nl = split3(norm)
    qh, ql, unused = split3(ends)
    norms = jnp.zeros((8, width), F32)
    first = 0 if is_rows else 3
    for k, piece in enumerate((nh, nm, nl)):
        norms = jnp.where(row == first + k, piece, norms)
    ones_at = (row >= 3) & (row < 6) if is_rows else row < 3
    norms = jnp.where(ones_at, 1.0, norms)
    if is_rows:
        h, m, l = -2.0 * h, -2.0 * m, -2.0 * l
        dist_rows = [h, h, m, h, l, m, norms]
        amp_rows = [qh, qh, ql]
    else:
        dist_rows = [h, m, h, l, h, m, norms]
        amp_rows = [qh, ql, qh]
    return dist_rows, amp_rows


def row_features(table, ids, lens, count_all):
    dist_rows, amp_rows = features(table, ids, lens, count_all, True)
    pad = jnp.zeros((48, ids.shape[1]), F32)
    return jnp.transpose(jnp.concatenate(dist_rows + amp_rows + [pad], 0)).astype(BF16)


def col_features(table, ids, lens, count_all):
    dist_rows, amp_rows = features(table, ids, lens, count_all, False)
    width = ids.shape[1]
    zeros = lambda rows: jnp.zeros((rows, width), F32)
    return (
        jnp.concatenate(dist_rows + [zeros(72)], 0).astype(BF16),
        jnp.concatenate([zeros(56)] + amp_rows + [zeros(48)], 0).astype(BF16),
    )


def tile_values(d2, weight):
    inv = lax.rsqrt(d2)
    dist = d2 * inv
    t = dist - ((dist + ROUNDER) - ROUNDER)
    u = t * t
    cosine = COS_C[4]
    for c in COS_C[3::-1]:
        cosine = cosine * u + c
    sine = SIN_C[4]
    for c in SIN_C[3::-1]:
        sine = sine * u + c
    amp = weight * inv
    return (amp * cosine).astype(BF16), ((amp * t) * sine).astype(BF16)


def far_tile(a, bd, bw, x):
    d2 = jnp.dot(a, bd, preferred_element_type=F32)
    weight = jnp.dot(a, bw, preferred_element_type=F32)
    kre, kim = tile_values(d2, weight)
    return lax.dot_general(jnp.concatenate([kre, kim], 0), x, NT, preferred_element_type=F32)


def padded_x(x, rhs, cpad):
    zeros = jnp.zeros((LANES - cpad, x.shape[-1]), BF16)
    rows = []
    for r in range(rhs):
        rows += [x[r], zeros]
    return jnp.concatenate(rows, 0)


def geometry_rows_kernel(count_all, tri_ref, ids_ref, len_ref, a_ref):
    a_ref[...] = row_features(make_table(tri_ref[...]), ids_ref[...], len_ref[...], count_all)


def geometry_cols_kernel(count_all, tri_ref, ids_ref, len_ref, bd_ref, bw_ref):
    bd, bw = col_features(make_table(tri_ref[...]), ids_ref[...], len_ref[...], count_all)
    bd_ref[...] = bd
    bw_ref[...] = bw


def geometry_call(tri, ids, lens, count_all, is_rows, chunk):
    width = ids.shape[1]
    in_specs = [
        pl.BlockSpec(tri.shape, lambda i: (0, 0)),
        pl.BlockSpec((2, chunk), lambda i: (0, i)),
        pl.BlockSpec((1, chunk), lambda i: (0, i)),
    ]
    if is_rows:
        kern = geometry_rows_kernel
        out_specs = pl.BlockSpec((chunk, LANES), lambda i: (i, 0))
        out_shape = jax.ShapeDtypeStruct((width, LANES), BF16)
    else:
        kern = geometry_cols_kernel
        out_specs = [pl.BlockSpec((LANES, chunk), lambda i: (0, i))] * 2
        out_shape = [jax.ShapeDtypeStruct((LANES, width), BF16)] * 2
    return pl.pallas_call(
        functools.partial(kern, count_all),
        grid=(width // chunk,),
        in_specs=in_specs,
        out_specs=out_specs,
        out_shape=out_shape,
        compiler_params=pltpu.CompilerParams(vmem_limit_bytes=VMEM_LIMIT),
    )(tri, ids, lens)


def near_into(acc_re, acc_im, x_full, col_ref, val_ref, block_count):
    row_blocks, per_tile = val_ref.shape[0], val_ref.shape[1]
    lane = lax.broadcasted_iota(jnp.int32, (BS, LANES), 1)

    def one(b, carry):
        total = jnp.zeros((2 * BS, x_full.shape[0]), F32)
        for j in range(per_tile):
            local = lax.rem(col_ref[b, j], block_count)
            pair = lax.div(local, 2)
            odd = lax.rem(local, 2) == 1
            value = val_ref[b, j].astype(F32)
            swapped = jnp.concatenate([value[:, BS:], value[:, :BS]], 1)
            keep = (lane >> 6) == lax.rem(local, 2)
            re_lhs = jnp.where(keep, jnp.where(odd, swapped, value), 0.0)
            im_lhs = jnp.where(keep, jnp.where(odd, value, swapped), 0.0)
            lhs = jnp.concatenate([re_lhs, im_lhs], 0).astype(BF16)
            cols = x_full[:, pl.ds(pl.multiple_of(pair * LANES, LANES), LANES)]
            total = total + lax.dot_general(lhs, cols, NT, preferred_element_type=F32)
        rows = pl.ds(pl.multiple_of(b * BS, BS), BS)
        acc_re[rows, :] = acc_re[rows, :] + total[:BS]
        acc_im[rows, :] = acc_im[rows, :] + total[BS:]
        return carry

    lax.fori_loop(0, row_blocks, one, 0)


def far_kernel(rhs, part_angles, mt, col_ref, a_ref, bd_ref, bw_ref, x_ref, own_ref, val_ref, y_ref, acc_re, acc_im, x_full):
    step = pl.program_id(0)
    cpad = x_ref.shape[2]

    @pl.when(step == 0)
    def _():
        acc_re[...] = jnp.zeros_like(acc_re)
        acc_im[...] = jnp.zeros_like(acc_im)
        x_full[...] = padded_x(own_ref[...], rhs, cpad)
        near_into(acc_re, acc_im, x_full, col_ref, val_ref, own_ref.shape[2] // BS)

    x = padded_x(x_ref[0], rhs, cpad)
    bd, bw = bd_ref[...], bw_ref[...]

    def rows_at(i, carry):
        rows = pl.ds(pl.multiple_of(i * mt, mt), mt)
        out = far_tile(a_ref[rows, :], bd, bw, x)
        acc_re[rows, :] = acc_re[rows, :] + out[:mt]
        acc_im[rows, :] = acc_im[rows, :] + out[mt:]
        return carry

    lax.fori_loop(0, ROWS_DEV // mt, rows_at, 0)

    @pl.when(step == pl.num_programs(0) - 1)
    def _():
        for r in range(rhs):
            lanes = slice(r * LANES, (r + 1) * LANES)
            re = jnp.transpose(acc_re[:, lanes])
            im = jnp.transpose(acc_im[:, lanes])
            pa = part_angles
            y_ref[r, 0:pa, :] = re[:pa] - im[pa : 2 * pa]
            y_ref[r, pa : 2 * pa, :] = re[pa : 2 * pa] + im[:pa]


def far_call(near_col, a, bd, bw, x_all, x_own, near_val, rhs, part_angles):
    groups, unused, cpad, tile = x_all.shape
    nt = 512 if tile % 512 == 0 else 128
    per_group = tile // nt
    mt = 256
    full = lambda array: pl.BlockSpec(array.shape, lambda i, col: (0,) * array.ndim)
    grid_spec = pltpu.PrefetchScalarGridSpec(
        num_scalar_prefetch=1,
        grid=(groups * per_group,),
        in_specs=[
            full(a),
            pl.BlockSpec((LANES, nt), lambda i, col: (0, i)),
            pl.BlockSpec((LANES, nt), lambda i, col: (0, i)),
            pl.BlockSpec((1, rhs, cpad, nt), lambda i, col: (i // per_group, 0, 0, i % per_group)),
            full(x_own),
            full(near_val),
        ],
        out_specs=pl.BlockSpec((rhs, 2 * part_angles, ROWS_DEV), lambda i, col: (0, 0, 0)),
        scratch_shapes=[
            pltpu.VMEM((ROWS_DEV, rhs * LANES), F32),
            pltpu.VMEM((ROWS_DEV, rhs * LANES), F32),
            pltpu.VMEM((rhs * LANES, tile), BF16),
        ],
    )
    return pl.pallas_call(
        functools.partial(far_kernel, rhs, part_angles, mt),
        grid_spec=grid_spec,
        out_shape=jax.ShapeDtypeStruct((rhs, 2 * part_angles, ROWS_DEV), F32),
        compiler_params=pltpu.CompilerParams(vmem_limit_bytes=VMEM_LIMIT),
    )(near_col, a, bd, bw, x_all, x_own, near_val)


def complex_pairs(real_part, imag_part, where_at):
    return jnp.stack(
        [jnp.stack([real_part, -imag_part], where_at), jnp.stack([imag_part, real_part], where_at)],
        where_at,
    )


def dual_apply(moved, dual_blocks):
    angle_count = moved.shape[1]
    row_blocks = dual_blocks.shape[0]
    blocked = moved.reshape(2, angle_count, row_blocks, BS)
    paired = complex_pairs(blocked[0], blocked[1], 0)
    operator = dual_blocks.reshape(row_blocks, BS, 2, BS)
    result = jnp.einsum("bmtn,otabn->oabm", operator, paired, preferred_element_type=jnp.float32)
    return result.reshape(2, angle_count, row_blocks * BS)


def body(currents, tri_cent, edge_tris, edge_len, near_col, near_val, refine_map, dual_blocks):
    blk_count = lax.axis_size("blk")
    rhs_count = lax.axis_size("rhs")
    sub_count = lax.axis_size("sub")
    blk_index = lax.axis_index("blk")
    rhs_index = lax.axis_index("rhs")
    sub_index = lax.axis_index("sub")
    angle_count = currents.shape[1]
    tile_cols = currents.shape[2]
    part_angles = angle_count // rhs_count
    group_cols = tile_cols * rhs_count
    count_all = group_cols * blk_count
    my_owner = blk_index * sub_count + sub_index
    first_row = my_owner * ROWS_DEV

    channels = 2 * part_angles
    cpad = -(-channels // 16) * 16
    x_own = jnp.transpose(
        currents.reshape(2, rhs_count, part_angles, tile_cols), (1, 0, 2, 3)
    ).reshape(rhs_count, channels, tile_cols)
    x_own = jnp.pad(x_own, ((0, 0), (0, cpad - channels), (0, 0)))
    x_all = lax.all_gather(x_own, "blk", axis=0, tiled=False)

    tri = tri_cent.reshape(-1, LANES)
    row_ids = lax.dynamic_slice_in_dim(edge_tris, first_row, ROWS_DEV, 1)
    row_len = lax.dynamic_slice_in_dim(edge_len, first_row, ROWS_DEV, 0)
    take_cols = lambda v, lead: lax.dynamic_index_in_dim(
        v.reshape(lead, blk_count, rhs_count, tile_cols), rhs_index, 2, False
    ).reshape(lead, blk_count * tile_cols)
    col_ids = take_cols(edge_tris, 2)
    col_len = take_cols(edge_len, 1)
    a = geometry_call(tri, row_ids, row_len[None], count_all, True, 512)
    bd, bw = geometry_call(tri, col_ids, col_len, count_all, False, 512)
    local_sum = far_call(near_col, a, bd, bw, x_all, x_own, near_val, rhs_count, part_angles)
    product = lax.psum_scatter(local_sum, "rhs", scatter_dimension=0, tiled=False)
    flat_rows = product.astype(jnp.bfloat16)
    owners = blk_count * sub_count
    slot_rows = ROWS_DEV // owners
    row_range = jnp.arange(ROWS_DEV, dtype=jnp.int32)
    owner_range = jnp.arange(owners, dtype=jnp.int32)
    earlier = (row_range[:, None] > row_range[None, :]).astype(jnp.bfloat16)
    own_map = lax.dynamic_slice_in_dim(refine_map, my_owner * ROWS_DEV, ROWS_DEV, 0)
    target_owner = own_map // ROWS_DEV
    owner_onehot = (target_owner[:, None] == owner_range[None, :]).astype(jnp.bfloat16)
    prior_counts = jnp.dot(earlier, owner_onehot, preferred_element_type=jnp.float32)
    send_rank = jnp.sum(prior_counts * owner_onehot.astype(jnp.float32), axis=1).astype(jnp.int32)
    send_slot = target_owner * slot_rows + send_rank
    send_perm = (send_slot[:, None] == row_range[None, :]).astype(jnp.bfloat16)
    outgoing = jnp.dot(flat_rows, send_perm, preferred_element_type=jnp.float32).astype(
        jnp.bfloat16
    )
    arrived = lax.all_to_all(
        outgoing.reshape(channels, owners, slot_rows),
        ("blk", "sub"),
        split_axis=1,
        concat_axis=1,
        tiled=True,
    )
    source_table = refine_map.reshape(owners, ROWS_DEV)
    bound_here = source_table // ROWS_DEV == my_owner
    recv_counts = jnp.dot(
        bound_here.astype(jnp.bfloat16), jnp.transpose(earlier), preferred_element_type=jnp.float32
    )
    recv_rank = recv_counts.astype(jnp.int32)
    landing = source_table % ROWS_DEV
    slot_range = jnp.arange(slot_rows, dtype=jnp.int32)
    matches = bound_here[:, :, None] & (recv_rank[:, :, None] == slot_range[None, None, :])
    slot_position = jnp.sum(jnp.where(matches, landing[:, :, None], 0), axis=1).reshape(ROWS_DEV)
    recv_perm = (slot_position[:, None] == row_range[None, :]).astype(jnp.bfloat16)
    moved = jnp.dot(
        arrived.reshape(channels, ROWS_DEV), recv_perm, preferred_element_type=jnp.float32
    ).astype(jnp.bfloat16)
    return dual_apply(moved.reshape(2, part_angles, ROWS_DEV), dual_blocks)


def solution(mesh):
    in_specs = (
        P(None, None, ("parts", "blk", "rhs")),
        P(None, "parts"),
        P(None, "parts"),
        P("parts"),
        P(("parts", "blk", "sub"), "rhs"),
        P(("parts", "blk", "sub"), "rhs", None, None),
        P("parts"),
        P(("parts", "blk", "sub"), None, None),
    )
    out_specs = P(None, "rhs", ("parts", "blk", "sub"))
    return jax.shard_map(body, mesh=mesh, in_specs=in_specs, out_specs=out_specs, check_vma=False)
```

```python
import functools
import math

import jax
import jax.numpy as jnp
from jax import lax
from jax.experimental import pallas as pl
from jax.experimental.pallas import tpu as pltpu
from jax.sharding import PartitionSpec as P

ROWS_DEV = 1536
BS = 64
LANES = 128
CENTER = 5.0
SOFT2 = 0.1 * 0.1
SPAN2 = 9.0
CHARGE_TERM = 0.5
COS_C = (0.99995979, -19.73104169, 64.67343113, -82.40355036, 45.64655658)
SIN_C = (6.2830558, -41.33121431, 81.36681529, -74.47800454, 32.78140079)
ROUNDER = 12582912.0

F32 = jnp.float32
BF16 = jnp.bfloat16
MESH = pl.DeviceIdType.MESH
NT = (((1,), (1,)), ((), ()))
VMEM_LIMIT = 56 * 1024 * 1024


def split3(x):
    h = x.astype(BF16).astype(F32)
    m = (x - h).astype(BF16).astype(F32)
    return h, m, (x - h - m).astype(BF16).astype(F32)


def lookup(table, ids):
    high = table.shape[0] // 3
    width = ids.shape[1]
    low_id = ids & (LANES - 1)
    high_id = ids >> 7
    lows = lax.broadcasted_iota(jnp.int32, (LANES, width), 0) == low_id
    onehot = jnp.where(lows, 1.0, 0.0).astype(BF16)
    picked = jnp.dot(
        table, jnp.concatenate([onehot] * 3, 0), preferred_element_type=F32
    )
    mask = lax.broadcasted_iota(jnp.int32, (high, width), 0) == high_id
    rows = [
        jnp.sum(jnp.where(mask, picked[c * high : (c + 1) * high], 0.0), axis=0, keepdims=True)
        for c in range(3)
    ]
    return jnp.concatenate(rows + [jnp.zeros((5, width), F32)], 0)


def make_table(tri):
    return jnp.concatenate([piece.astype(BF16) for piece in split3(tri)], 1)


def features(table, ids, lens, count_all, is_rows):
    width = ids.shape[1]
    plus, minus = lookup(table, ids[0:1]), lookup(table, ids[1:2])
    row = lax.broadcasted_iota(jnp.int32, (8, width), 0)
    pos = jnp.where(row < 3, 0.5 * (plus + minus) - CENTER, 0.0)
    norm = jnp.sum(pos * pos, axis=0, keepdims=True)
    ends = (minus - plus) * lens + jnp.where(row == 3, lens, 0.0)
    if is_rows:
        scale = 1.0
    else:
        norm = norm + SOFT2
        scale = jnp.where(row == 3, -CHARGE_TERM, 1.0 / SPAN2) / math.sqrt(count_all)
    ends = ends * scale
    h, m, l = split3(pos)
    nh, nm, nl = split3(norm)
    qh, ql, unused = split3(ends)
    norms = jnp.zeros((8, width), F32)
    first = 0 if is_rows else 3
    for k, piece in enumerate((nh, nm, nl)):
        norms = jnp.where(row == first + k, piece, norms)
    ones_at = (row >= 3) & (row < 6) if is_rows else row < 3
    norms = jnp.where(ones_at, 1.0, norms)
    if is_rows:
        h, m, l = -2.0 * h, -2.0 * m, -2.0 * l
        dist_rows = [h, h, m, h, l, m, norms]
        amp_rows = [qh, qh, ql]
    else:
        dist_rows = [h, m, h, l, h, m, norms]
        amp_rows = [qh, ql, qh]
    return dist_rows, amp_rows


def row_features(table, ids, lens, count_all):
    dist_rows, amp_rows = features(table, ids, lens, count_all, True)
    pad = jnp.zeros((48, ids.shape[1]), F32)
    return jnp.transpose(jnp.concatenate(dist_rows + amp_rows + [pad], 0)).astype(BF16)


def col_features(table, ids, lens, count_all):
    dist_rows, amp_rows = features(table, ids, lens, count_all, False)
    width = ids.shape[1]
    zeros = lambda rows: jnp.zeros((rows, width), F32)
    return (
        jnp.concatenate(dist_rows + [zeros(72)], 0).astype(BF16),
        jnp.concatenate([zeros(56)] + amp_rows + [zeros(48)], 0).astype(BF16),
    )


def tile_values(d2, weight):
    inv = lax.rsqrt(d2)
    dist = d2 * inv
    t = dist - ((dist + ROUNDER) - ROUNDER)
    u = t * t
    cosine = COS_C[4]
    for c in COS_C[3::-1]:
        cosine = cosine * u + c
    sine = SIN_C[4]
    for c in SIN_C[3::-1]:
        sine = sine * u + c
    amp = weight * inv
    return (amp * cosine).astype(BF16), ((amp * t) * sine).astype(BF16)


def far_tile(a, bd, bw, x):
    d2 = jnp.dot(a, bd, preferred_element_type=F32)
    weight = jnp.dot(a, bw, preferred_element_type=F32)
    kre, kim = tile_values(d2, weight)
    return lax.dot_general(jnp.concatenate([kre, kim], 0), x, NT, preferred_element_type=F32)


def combine(real_rows, imag_rows, part_angles):
    lane = lax.broadcasted_iota(jnp.int32, real_rows.shape, 1)
    ahead = pltpu.roll(imag_rows, LANES - part_angles, 1)
    behind = pltpu.roll(imag_rows, part_angles, 1)
    turned = jnp.where(lane < part_angles, -ahead, jnp.where(lane < 2 * part_angles, behind, 0.0))
    return real_rows + turned


def send_slots(own_map, owners):
    width = own_map.shape[1]
    slot_rows = width // owners
    target = lax.div(own_map, jnp.int32(ROWS_DEV))
    before = lax.broadcasted_iota(jnp.int32, (LANES, LANES), 0) < lax.broadcasted_iota(
        jnp.int32, (LANES, LANES), 1
    )
    triangle = jnp.where(before, 1.0, 0.0).astype(BF16)
    running = jnp.zeros((owners, 1), F32)
    ranks = []
    for k in range(width // LANES):
        part = target[:, k * LANES : (k + 1) * LANES]
        hits = lax.broadcasted_iota(jnp.int32, (owners, LANES), 0) == part
        onehot = jnp.where(hits, 1.0, 0.0)
        prior = running + jnp.dot(onehot.astype(BF16), triangle, preferred_element_type=F32)
        ranks.append(jnp.sum(onehot * prior, axis=0, keepdims=True))
        running = running + jnp.sum(onehot, axis=1, keepdims=True)
    return target * slot_rows + jnp.concatenate(ranks, 1).astype(jnp.int32)


def near_kernel(part_angles, col_ref, own_ref, val_ref, y_ref, x_pad, re_buf, im_buf):
    rhs_count, cpad, tile = own_ref.shape
    row_blocks, per_row = val_ref.shape[0], val_ref.shape[1]
    lane = lax.broadcasted_iota(jnp.int32, (BS, LANES), 1)
    if cpad < LANES:
        x_pad[:, cpad:, :] = jnp.zeros((rhs_count, LANES - cpad, tile), BF16)
    x_pad[:, 0:cpad, :] = own_ref[...]

    def near_block(i, carry):
        total = jnp.zeros((2 * BS, rhs_count * LANES), F32)
        for j in range(per_row):
            local = lax.rem(col_ref[i, j], tile // BS)
            odd = lax.rem(local, 2)
            pair = lax.div(local, 2)
            value = val_ref[i, j].astype(F32)
            swapped = jnp.concatenate([value[:, BS:], value[:, :BS]], 1)
            keep = (lane >> 6) == odd
            re_lhs = jnp.where(keep, jnp.where(odd == 1, swapped, value), 0.0)
            im_lhs = jnp.where(keep, jnp.where(odd == 1, value, swapped), 0.0)
            lhs = jnp.concatenate([re_lhs, im_lhs], 0).astype(BF16)
            cols = x_pad[:, :, pl.ds(pl.multiple_of(pair * LANES, LANES), LANES)]
            cols = cols.reshape(rhs_count * LANES, LANES)
            total = total + lax.dot_general(lhs, cols, NT, preferred_element_type=F32)
        rows = pl.ds(pl.multiple_of(i * BS, BS), BS)
        re_buf[rows, :] = total[:BS]
        im_buf[rows, :] = total[BS:]
        return carry

    lax.fori_loop(0, row_blocks, near_block, 0, unroll=4)
    for q in range(rhs_count):
        lanes = slice(q * LANES, (q + 1) * LANES)
        y_ref[q] = combine(re_buf[:, lanes], im_buf[:, lanes], part_angles)


def near_call(near_col, x_own, near_val, part_angles):
    rhs_count, unused, tile = x_own.shape
    vmem = pl.BlockSpec(memory_space=pltpu.VMEM)
    return pl.pallas_call(
        functools.partial(near_kernel, part_angles),
        out_shape=jax.ShapeDtypeStruct((rhs_count, ROWS_DEV, LANES), F32),
        in_specs=[pl.BlockSpec(memory_space=pltpu.SMEM), vmem, vmem],
        out_specs=vmem,
        scratch_shapes=[
            pltpu.VMEM((rhs_count, LANES, tile), BF16),
            pltpu.VMEM((ROWS_DEV, rhs_count * LANES), F32),
            pltpu.VMEM((ROWS_DEV, rhs_count * LANES), F32),
        ],
        compiler_params=pltpu.CompilerParams(vmem_limit_bytes=VMEM_LIMIT),
    )(near_col, x_own, near_val)


def whole_kernel(
    sizes, part_angles,
    tri_ref, row_ids_ref, row_len_ref, col_ids_ref, col_len_ref, own_ref, near_ref, map_ref, dual_ref,
    out_ref,
    a_buf, bd_buf, bw_buf, x_all, acc_re, acc_im, y_own, y_send, y_recv, go_buf, come_buf,
    ag_send, ag_recv, fw_send, fw_recv, y_ssem, y_rsem, p_send, p_recv,
):
    blk_count, rhs_count, sub_count = sizes
    b, r, s = (lax.axis_index(name) for name in ("blk", "rhs", "sub"))
    cpad, tile = own_ref.shape[1], own_ref.shape[2]
    owners = blk_count * sub_count
    me = b * sub_count + s
    count_all = blk_count * rhs_count * tile
    half = rhs_count // sub_count
    slot_rows = ROWS_DEV // owners
    mt = 512
    chunks = ROWS_DEV // mt
    nt = 512 if tile % 512 == 0 else LANES
    per_tile = tile // nt

    barrier = pltpu.get_barrier_semaphore()

    def greet_owner(k, carry):
        o = lax.rem(me + k, owners)
        pl.semaphore_signal(
            barrier, inc=1,
            device_id={"blk": lax.div(o, sub_count), "sub": lax.rem(o, sub_count)},
            device_id_type=MESH,
        )
        return carry

    def greet_rhs(k, carry):
        pl.semaphore_signal(
            barrier, inc=1, device_id={"rhs": lax.rem(r + k, rhs_count)}, device_id_type=MESH
        )
        return carry

    lax.fori_loop(1, owners, greet_owner, 0)
    lax.fori_loop(1, rhs_count, greet_rhs, 0)
    pl.semaphore_wait(barrier, owners - 1 + rhs_count - 1)

    mine = pl.ds(s * half, half)
    theirs = pl.ds((1 - s) * half, half)
    real = pl.ds(0, cpad)

    def gather_copy(k):
        return pltpu.make_async_remote_copy(
            src_ref=own_ref.at[mine],
            dst_ref=x_all.at[b, mine, real],
            send_sem=ag_send.at[k], recv_sem=ag_recv.at[k],
            device_id={"blk": lax.rem(b + k, blk_count)}, device_id_type=MESH,
        )

    def gather_arrival(k):
        source = lax.rem(b - k + blk_count, blk_count)
        return pltpu.make_async_remote_copy(
            src_ref=own_ref.at[mine],
            dst_ref=x_all.at[source, mine, real],
            send_sem=ag_send.at[k], recv_sem=ag_recv.at[k],
            device_id={"blk": source}, device_id_type=MESH,
        )

    def pass_on(k, which):
        source = lax.rem(b - k + blk_count, blk_count)
        return pltpu.make_async_remote_copy(
            src_ref=x_all.at[source, which, real],
            dst_ref=x_all.at[source, which, real],
            send_sem=fw_send.at[k], recv_sem=fw_recv.at[k],
            device_id={"sub": 1 - s}, device_id_type=MESH,
        )

    def start_gather(k, carry):
        gather_copy(k).start()
        return carry

    lax.fori_loop(1, blk_count, start_gather, 0)

    if cpad < LANES:
        x_all[:, :, cpad:, :] = jnp.zeros((blk_count, rhs_count, LANES - cpad, tile), BF16)
    x_all[b, :, 0:cpad, :] = own_ref[...]
    acc_re[...] = jnp.zeros_like(acc_re)
    acc_im[...] = jnp.zeros_like(acc_im)

    table = make_table(tri_ref[...])
    gw = nt

    def row_geometry(i, carry):
        at = pl.ds(pl.multiple_of(i * 512, 512), 512)
        a_buf[at, :] = row_features(table, row_ids_ref[:, at], row_len_ref[:, at], count_all)
        return carry

    lax.fori_loop(0, ROWS_DEV // 512, row_geometry, 0)

    def col_geometry(i, carry):
        at = pl.ds(pl.multiple_of(i * gw, gw), gw)
        bd, bw = col_features(table, col_ids_ref[:, at], col_len_ref[:, at], count_all)
        bd_buf[:, at] = bd
        bw_buf[:, at] = bw
        return carry

    lax.fori_loop(0, blk_count * per_tile, col_geometry, 0)

    def far_step(group, n, rows):
        at = pl.ds(pl.multiple_of(n * nt, nt), nt)
        feats = pl.ds(pl.multiple_of(group * tile + n * nt, nt), nt)
        x = x_all[group, :, :, at].reshape(rhs_count * LANES, nt)
        out = far_tile(a_buf[rows, :], bd_buf[:, feats], bw_buf[:, feats], x)
        acc_re[rows, :] = acc_re[rows, :] + out[:mt]
        acc_im[rows, :] = acc_im[rows, :] + out[mt:]

    def own_tile(i, carry):
        rows = pl.ds(pl.multiple_of(lax.rem(i, chunks) * mt, mt), mt)
        far_step(b, lax.div(i, chunks), rows)
        return carry

    lax.fori_loop(0, per_tile * chunks, own_tile, 0)

    def forward(k, carry):
        gather_arrival(k).wait_recv()
        pass_on(k, mine).start()
        return carry

    lax.fori_loop(1, blk_count, forward, 0)

    def forwarded(k, carry):
        gather_copy(k).wait_send()
        pass_on(k, mine).wait_send()
        pass_on(k, theirs).wait_recv()
        return carry

    lax.fori_loop(1, blk_count, forwarded, 0)

    def y_copy(c, k, outbound):
        rows = pl.ds(pl.multiple_of(c * mt, mt), mt)
        other = lax.rem(r + k, rhs_count) if outbound else lax.rem(r - k + rhs_count, rhs_count)
        return pltpu.make_async_remote_copy(
            src_ref=y_send.at[other, rows],
            dst_ref=y_recv.at[r if outbound else other, rows],
            send_sem=y_ssem.at[c, k], recv_sem=y_rsem.at[c, k],
            device_id={"rhs": other}, device_id_type=MESH,
        )

    def row_chunk(c, carry):
        rows = pl.ds(pl.multiple_of(c * mt, mt), mt)

        def column(i, inner):
            group = lax.rem(b + 1 + lax.div(i, per_tile), blk_count)
            far_step(group, lax.rem(i, per_tile), rows)
            return inner

        lax.fori_loop(0, (blk_count - 1) * per_tile, column, 0)
        own = jnp.zeros((mt, LANES), F32)
        for q in range(rhs_count):
            lanes = slice(q * LANES, (q + 1) * LANES)
            y = combine(acc_re[rows, lanes], acc_im[rows, lanes], part_angles) + near_ref[q, rows, :]
            y_send[q, rows, :] = y.astype(BF16)
            own = own + jnp.where(r == q, y, 0.0)
        y_own[rows, :] = own

        def start(k, inner):
            y_copy(c, k, True).start()
            return inner

        lax.fori_loop(1, rhs_count, start, 0)
        return carry

    lax.fori_loop(0, chunks, row_chunk, 0)

    own_map = map_ref[...]
    slots = send_slots(own_map, owners)
    place = lax.rem(own_map, jnp.int32(ROWS_DEV))
    sub_row = lax.broadcasted_iota(jnp.int32, (LANES, ROWS_DEV), 0)
    marks = jnp.where(
        sub_row == 2 * part_angles,
        place >> 6,
        jnp.where(sub_row == 2 * part_angles + 1, place & 63, 0),
    )
    total = y_own[...] + jnp.transpose(marks.astype(F32))

    for c in range(chunks):
        for k in range(1, rhs_count):
            y_copy(c, k, True).wait_send()
            y_copy(c, k, False).wait_recv()
    for k in range(1, rhs_count):
        total = total + y_recv[lax.rem(r - k + rhs_count, rhs_count)].astype(F32)
    flat = total.astype(BF16)

    def owner_copy(k, outbound):
        o = lax.rem(me + k, owners) if outbound else lax.rem(me - k + owners, owners)
        return pltpu.make_async_remote_copy(
            src_ref=go_buf.at[o],
            dst_ref=come_buf.at[me if outbound else o],
            send_sem=p_send.at[k], recv_sem=p_recv.at[k],
            device_id={"blk": lax.div(o, sub_count), "sub": lax.rem(o, sub_count)},
            device_id_type=MESH,
        )

    def outgoing(o):
        at = lax.broadcasted_iota(jnp.int32, (slot_rows, ROWS_DEV), 0) + o * slot_rows
        perm = jnp.where(at == slots, 1.0, 0.0).astype(BF16)
        return jnp.dot(perm, flat, preferred_element_type=F32).astype(BF16)

    def send_owner(k, carry):
        o = lax.rem(me + k, owners)
        go_buf[o] = outgoing(o)
        owner_copy(k, True).start()
        return carry

    lax.fori_loop(1, owners, send_owner, 0)
    come_buf[me] = outgoing(me)

    def owner_done(k, carry):
        owner_copy(k, True).wait_send()
        owner_copy(k, False).wait_recv()
        return carry

    lax.fori_loop(1, owners, owner_done, 0)

    arrived = come_buf[...].reshape(ROWS_DEV, LANES)
    turned = jnp.transpose(arrived.astype(F32))
    spot = turned[2 * part_angles : 2 * part_angles + 1] * 64.0 + turned[2 * part_angles + 1 : 2 * part_angles + 2]
    spot = spot.astype(jnp.int32)
    wide = 256

    def landing(i, carry):
        at = lax.broadcasted_iota(jnp.int32, (wide, ROWS_DEV), 0) + i * wide
        perm = jnp.where(at == spot, 1.0, 0.0).astype(BF16)
        moved = jnp.dot(perm, arrived, preferred_element_type=F32).astype(BF16)
        rows = []
        for q in range(wide // BS):
            value = dual_ref[i * (wide // BS) + q]
            piece = moved[q * BS : (q + 1) * BS]
            re = jnp.dot(value[:, :BS], piece, preferred_element_type=F32)
            im = jnp.dot(value[:, BS:], piece, preferred_element_type=F32)
            rows.append(combine(re, im, part_angles))
        result = jnp.transpose(jnp.concatenate(rows, 0))
        cols = pl.ds(pl.multiple_of(i * wide, wide), wide)
        out_ref[0, :, cols] = result[:part_angles]
        out_ref[1, :, cols] = result[part_angles : 2 * part_angles]
        return carry

    lax.fori_loop(0, ROWS_DEV // wide, landing, 0)


def body(currents, tri_cent, edge_tris, edge_len, near_col, near_val, refine_map, dual_blocks):
    blk_count = lax.axis_size("blk")
    rhs_count = lax.axis_size("rhs")
    sub_count = lax.axis_size("sub")
    rhs_index = lax.axis_index("rhs")
    angle_count, tile = currents.shape[1], currents.shape[2]
    part_angles = angle_count // rhs_count
    owners = blk_count * sub_count
    first_row = (lax.axis_index("blk") * sub_count + lax.axis_index("sub")) * ROWS_DEV

    channels = 2 * part_angles
    cpad = -(-channels // 16) * 16
    x_own = jnp.transpose(
        currents.reshape(2, rhs_count, part_angles, tile), (1, 0, 2, 3)
    ).reshape(rhs_count, channels, tile)
    x_own = jnp.pad(x_own, ((0, 0), (0, cpad - channels), (0, 0)))

    tri = tri_cent.reshape(-1, LANES)
    row_ids = lax.dynamic_slice_in_dim(edge_tris, first_row, ROWS_DEV, 1)
    row_len = lax.dynamic_slice_in_dim(edge_len, first_row, ROWS_DEV, 0)[None]
    own_map = lax.dynamic_slice_in_dim(refine_map, first_row, ROWS_DEV, 0)[None]
    take_cols = lambda v, lead: lax.dynamic_index_in_dim(
        v.reshape(lead, blk_count, rhs_count, tile), rhs_index, 2, False
    ).reshape(lead, blk_count * tile)
    col_ids = take_cols(edge_tris, 2)
    col_len = take_cols(edge_len, 1)
    near_sum = near_call(near_col, x_own, near_val, part_angles)
    wide = rhs_count * LANES
    chunks = ROWS_DEV // 512
    vmem = pl.BlockSpec(memory_space=pltpu.VMEM)
    dma = lambda *shape: pltpu.SemaphoreType.DMA(shape)
    return pl.pallas_call(
        functools.partial(whole_kernel, (blk_count, rhs_count, sub_count), part_angles),
        out_shape=jax.ShapeDtypeStruct((2, part_angles, ROWS_DEV), F32),
        in_specs=[vmem] * 9,
        out_specs=vmem,
        scratch_shapes=[
            pltpu.VMEM((ROWS_DEV, LANES), BF16),
            pltpu.VMEM((LANES, blk_count * tile), BF16),
            pltpu.VMEM((LANES, blk_count * tile), BF16),
            pltpu.VMEM((blk_count, rhs_count, LANES, tile), BF16),
            pltpu.VMEM((ROWS_DEV, wide), F32),
            pltpu.VMEM((ROWS_DEV, wide), F32),
            pltpu.VMEM((ROWS_DEV, LANES), F32),
            pltpu.VMEM((rhs_count, ROWS_DEV, LANES), BF16),
            pltpu.VMEM((rhs_count, ROWS_DEV, LANES), BF16),
            pltpu.VMEM((owners, ROWS_DEV // owners, LANES), BF16),
            pltpu.VMEM((owners, ROWS_DEV // owners, LANES), BF16),
            dma(blk_count), dma(blk_count), dma(blk_count), dma(blk_count),
            dma(chunks, rhs_count), dma(chunks, rhs_count), dma(owners), dma(owners),
        ],
        compiler_params=pltpu.CompilerParams(
            collective_id=0, has_side_effects=True, vmem_limit_bytes=VMEM_LIMIT
        ),
    )(tri, row_ids, row_len, col_ids, col_len, x_own, near_sum, own_map, dual_blocks)


def solution(mesh):
    in_specs = (
        P(None, None, ("parts", "blk", "rhs")),
        P(None, "parts"),
        P(None, "parts"),
        P("parts"),
        P(("parts", "blk", "sub"), "rhs"),
        P(("parts", "blk", "sub"), "rhs", None, None),
        P("parts"),
        P(("parts", "blk", "sub"), None, None),
    )
    out_specs = P(None, "rhs", ("parts", "blk", "sub"))
    return jax.shard_map(body, mesh=mesh, in_specs=in_specs, out_specs=out_specs, check_vma=False)
```

```python
import functools
import math

import jax
import jax.numpy as jnp
from jax import lax
from jax.experimental import pallas as pl
from jax.experimental.pallas import tpu as pltpu
from jax.sharding import PartitionSpec as P

ROWS_DEV = 1536
BS = 64
LANES = 128
CENTER = 5.0
SOFT2 = 0.1 * 0.1
SPAN2 = 9.0
CHARGE_TERM = 0.5
COS_C = (0.99995979, -19.73104169, 64.67343113, -82.40355036, 45.64655658)
SIN_C = (6.2830558, -41.33121431, 81.36681529, -74.47800454, 32.78140079)
ROUNDER = 12582912.0

F32 = jnp.float32
BF16 = jnp.bfloat16
MESH = pl.DeviceIdType.MESH
NT = (((1,), (1,)), ((), ()))
VMEM_LIMIT = 56 * 1024 * 1024


def split3(x):
    h = x.astype(BF16).astype(F32)
    m = (x - h).astype(BF16).astype(F32)
    return h, m, (x - h - m).astype(BF16).astype(F32)


def lookup(table, ids):
    high = table.shape[0] // 3
    width = ids.shape[1]
    low_id = ids & (LANES - 1)
    high_id = ids >> 7
    lows = lax.broadcasted_iota(jnp.int32, (LANES, width), 0) == low_id
    onehot = jnp.where(lows, 1.0, 0.0).astype(BF16)
    picked = jnp.dot(
        table, jnp.concatenate([onehot] * 3, 0), preferred_element_type=F32
    )
    mask = lax.broadcasted_iota(jnp.int32, (high, width), 0) == high_id
    rows = [
        jnp.sum(jnp.where(mask, picked[c * high : (c + 1) * high], 0.0), axis=0, keepdims=True)
        for c in range(3)
    ]
    return jnp.concatenate(rows + [jnp.zeros((5, width), F32)], 0)


def make_table(tri):
    return jnp.concatenate([piece.astype(BF16) for piece in split3(tri)], 1)


def features(table, ids, lens, count_all, is_rows):
    width = ids.shape[1]
    plus, minus = lookup(table, ids[0:1]), lookup(table, ids[1:2])
    row = lax.broadcasted_iota(jnp.int32, (8, width), 0)
    pos = jnp.where(row < 3, 0.5 * (plus + minus) - CENTER, 0.0)
    norm = jnp.sum(pos * pos, axis=0, keepdims=True)
    ends = (minus - plus) * lens + jnp.where(row == 3, lens, 0.0)
    if is_rows:
        scale = 1.0
    else:
        norm = norm + SOFT2
        scale = jnp.where(row == 3, -CHARGE_TERM, 1.0 / SPAN2) / math.sqrt(count_all)
    ends = ends * scale
    h, m, l = split3(pos)
    nh, nm, nl = split3(norm)
    qh, ql, unused = split3(ends)
    norms = jnp.zeros((8, width), F32)
    first = 0 if is_rows else 3
    for k, piece in enumerate((nh, nm, nl)):
        norms = jnp.where(row == first + k, piece, norms)
    ones_at = (row >= 3) & (row < 6) if is_rows else row < 3
    norms = jnp.where(ones_at, 1.0, norms)
    if is_rows:
        h, m, l = -2.0 * h, -2.0 * m, -2.0 * l
        dist_rows = [h, h, m, h, l, m, norms]
        amp_rows = [qh, qh, ql]
    else:
        dist_rows = [h, m, h, l, h, m, norms]
        amp_rows = [qh, ql, qh]
    return dist_rows, amp_rows


def row_features(table, ids, lens, count_all):
    dist_rows, amp_rows = features(table, ids, lens, count_all, True)
    pad = jnp.zeros((48, ids.shape[1]), F32)
    return jnp.transpose(jnp.concatenate(dist_rows + amp_rows + [pad], 0)).astype(BF16)


def col_features(table, ids, lens, count_all):
    dist_rows, amp_rows = features(table, ids, lens, count_all, False)
    width = ids.shape[1]
    zeros = lambda rows: jnp.zeros((rows, width), F32)
    return (
        jnp.concatenate(dist_rows + [zeros(72)], 0).astype(BF16),
        jnp.concatenate([zeros(56)] + amp_rows + [zeros(48)], 0).astype(BF16),
    )


def tile_values(d2, weight):
    inv = lax.rsqrt(d2)
    dist = d2 * inv
    t = dist - ((dist + ROUNDER) - ROUNDER)
    u = t * t
    cosine = COS_C[4]
    for c in COS_C[3::-1]:
        cosine = cosine * u + c
    sine = SIN_C[4]
    for c in SIN_C[3::-1]:
        sine = sine * u + c
    amp = weight * inv
    return (amp * cosine).astype(BF16), ((amp * t) * sine).astype(BF16)


def far_tile(a, bd, bw, x):
    d2 = jnp.dot(a, bd, preferred_element_type=F32)
    weight = jnp.dot(a, bw, preferred_element_type=F32)
    kre, kim = tile_values(d2, weight)
    return lax.dot_general(jnp.concatenate([kre, kim], 0), x, NT, preferred_element_type=F32)


def combine(real_rows, imag_rows, part_angles):
    lane = lax.broadcasted_iota(jnp.int32, real_rows.shape, 1)
    ahead = pltpu.roll(imag_rows, LANES - part_angles, 1)
    behind = pltpu.roll(imag_rows, part_angles, 1)
    turned = jnp.where(lane < part_angles, -ahead, jnp.where(lane < 2 * part_angles, behind, 0.0))
    return real_rows + turned


def send_slots(own_map, owners):
    width = own_map.shape[1]
    slot_rows = width // owners
    target = lax.div(own_map, jnp.int32(ROWS_DEV))
    before = lax.broadcasted_iota(jnp.int32, (LANES, LANES), 0) < lax.broadcasted_iota(
        jnp.int32, (LANES, LANES), 1
    )
    triangle = jnp.where(before, 1.0, 0.0).astype(BF16)
    running = jnp.zeros((owners, 1), F32)
    ranks = []
    for k in range(width // LANES):
        part = target[:, k * LANES : (k + 1) * LANES]
        hits = lax.broadcasted_iota(jnp.int32, (owners, LANES), 0) == part
        onehot = jnp.where(hits, 1.0, 0.0)
        prior = running + jnp.dot(onehot.astype(BF16), triangle, preferred_element_type=F32)
        ranks.append(jnp.sum(onehot * prior, axis=0, keepdims=True))
        running = running + jnp.sum(onehot, axis=1, keepdims=True)
    return target * slot_rows + jnp.concatenate(ranks, 1).astype(jnp.int32)


def near_kernel(part_angles, col_ref, cur_ref, val_ref, y_ref, x_ref, x_pad, re_buf, im_buf):
    rhs_count, cpad, tile = x_ref.shape
    row_blocks, per_row = val_ref.shape[0], val_ref.shape[1]
    lane = lax.broadcasted_iota(jnp.int32, (BS, LANES), 1)
    pa = part_angles
    for q in range(rhs_count):
        pieces = [cur_ref[t, q * pa : (q + 1) * pa, :].astype(F32) for t in range(2)]
        pieces.append(jnp.zeros((LANES - 2 * pa, tile), F32))
        x_pad[q] = jnp.concatenate(pieces, 0).astype(BF16)
    x_ref[...] = x_pad[:, 0:cpad, :]

    def near_block(i, carry):
        total = jnp.zeros((2 * BS, rhs_count * LANES), F32)
        for j in range(per_row):
            local = lax.rem(col_ref[i, j], tile // BS)
            odd = lax.rem(local, 2)
            pair = lax.div(local, 2)
            value = val_ref[i, j].astype(F32)
            swapped = jnp.concatenate([value[:, BS:], value[:, :BS]], 1)
            keep = (lane >> 6) == odd
            re_lhs = jnp.where(keep, jnp.where(odd == 1, swapped, value), 0.0)
            im_lhs = jnp.where(keep, jnp.where(odd == 1, value, swapped), 0.0)
            lhs = jnp.concatenate([re_lhs, im_lhs], 0).astype(BF16)
            cols = x_pad[:, :, pl.ds(pl.multiple_of(pair * LANES, LANES), LANES)]
            cols = cols.reshape(rhs_count * LANES, LANES)
            total = total + lax.dot_general(lhs, cols, NT, preferred_element_type=F32)
        rows = pl.ds(pl.multiple_of(i * BS, BS), BS)
        re_buf[rows, :] = total[:BS]
        im_buf[rows, :] = total[BS:]
        return carry

    lax.fori_loop(0, row_blocks, near_block, 0, unroll=4)
    for q in range(rhs_count):
        lanes = slice(q * LANES, (q + 1) * LANES)
        y_ref[q] = combine(re_buf[:, lanes], im_buf[:, lanes], part_angles)


def near_call(near_col, currents, near_val, rhs_count, cpad):
    unused, angle_count, tile = currents.shape
    vmem = pl.BlockSpec(memory_space=pltpu.VMEM)
    return pl.pallas_call(
        functools.partial(near_kernel, angle_count // rhs_count),
        out_shape=[
            jax.ShapeDtypeStruct((rhs_count, ROWS_DEV, LANES), F32),
            jax.ShapeDtypeStruct((rhs_count, cpad, tile), BF16),
        ],
        in_specs=[pl.BlockSpec(memory_space=pltpu.SMEM), vmem, vmem],
        out_specs=[vmem, vmem],
        scratch_shapes=[
            pltpu.VMEM((rhs_count, LANES, tile), BF16),
            pltpu.VMEM((ROWS_DEV, rhs_count * LANES), F32),
            pltpu.VMEM((ROWS_DEV, rhs_count * LANES), F32),
        ],
        compiler_params=pltpu.CompilerParams(vmem_limit_bytes=VMEM_LIMIT),
    )(near_col, currents, near_val)


def whole_kernel(
    sizes, part_angles,
    tri_ref, ids_ref, len_ref, own_ref, near_ref, map_ref, dual_ref,
    out_ref,
    a_buf, bd_buf, bw_buf, x_all, acc_re, acc_im, y_own, y_send, y_recv, go_buf, come_buf,
    ag_send, ag_recv, fw_send, fw_recv, y_ssem, y_rsem, p_send, p_recv, tri_buf,
):
    blk_count, rhs_count, sub_count = sizes
    b, r, s = (lax.axis_index(name) for name in ("blk", "rhs", "sub"))
    cpad, tile = own_ref.shape[1], own_ref.shape[2]
    owners = blk_count * sub_count
    me = b * sub_count + s
    count_all = blk_count * rhs_count * tile
    half = rhs_count // sub_count
    slot_rows = ROWS_DEV // owners
    mt = 512
    chunks = ROWS_DEV // mt
    nt = tile
    per_tile = 1

    barrier = pltpu.get_barrier_semaphore()

    def greet_owner(k, carry):
        o = lax.rem(me + k, owners)
        pl.semaphore_signal(
            barrier, inc=1,
            device_id={"blk": lax.div(o, sub_count), "sub": lax.rem(o, sub_count)},
            device_id_type=MESH,
        )
        return carry

    def greet_rhs(k, carry):
        pl.semaphore_signal(
            barrier, inc=1, device_id={"rhs": lax.rem(r + k, rhs_count)}, device_id_type=MESH
        )
        return carry

    lax.fori_loop(1, owners, greet_owner, 0)
    lax.fori_loop(1, rhs_count, greet_rhs, 0)
    pl.semaphore_wait(barrier, owners - 1 + rhs_count - 1)

    mine = pl.ds(s * half, half)
    theirs = pl.ds((1 - s) * half, half)
    real = pl.ds(0, cpad)

    def gather_copy(k):
        return pltpu.make_async_remote_copy(
            src_ref=own_ref.at[mine],
            dst_ref=x_all.at[b, mine, real],
            send_sem=ag_send.at[k], recv_sem=ag_recv.at[k],
            device_id={"blk": lax.rem(b + k, blk_count)}, device_id_type=MESH,
        )

    def gather_arrival(k):
        source = lax.rem(b - k + blk_count, blk_count)
        return pltpu.make_async_remote_copy(
            src_ref=own_ref.at[mine],
            dst_ref=x_all.at[source, mine, real],
            send_sem=ag_send.at[k], recv_sem=ag_recv.at[k],
            device_id={"blk": source}, device_id_type=MESH,
        )

    def pass_on(k, which):
        source = lax.rem(b - k + blk_count, blk_count)
        return pltpu.make_async_remote_copy(
            src_ref=x_all.at[source, which, real],
            dst_ref=x_all.at[source, which, real],
            send_sem=fw_send.at[k], recv_sem=fw_recv.at[k],
            device_id={"sub": 1 - s}, device_id_type=MESH,
        )

    def start_gather(k, carry):
        gather_copy(k).start()
        return carry

    lax.fori_loop(1, blk_count, start_gather, 0)

    if cpad < LANES:
        x_all[:, :, cpad:, :] = jnp.zeros((blk_count, rhs_count, LANES - cpad, tile), BF16)
    x_all[b, :, 0:cpad, :] = own_ref[...]
    acc_re[...] = jnp.zeros_like(acc_re)
    acc_im[...] = jnp.zeros_like(acc_im)

    high = tri_ref.shape[1] // LANES
    for c in range(3):
        for h in range(high):
            tri_buf[c * high + h : c * high + h + 1, :] = tri_ref[c : c + 1, h * LANES : (h + 1) * LANES]
    table = make_table(tri_buf[...])
    gw = 512 if tile % 512 == 0 else LANES
    per_geometry = tile // gw

    def row_geometry(i, carry):
        at = pl.ds(pl.multiple_of(i * 512, 512), 512)
        full = pl.ds(pl.multiple_of(me * ROWS_DEV + i * 512, 512), 512)
        a_buf[at, :] = row_features(table, ids_ref[:, full], len_ref[:, full], count_all)
        return carry

    lax.fori_loop(0, ROWS_DEV // 512, row_geometry, 0)

    def col_geometry(i, carry):
        at = pl.ds(pl.multiple_of(i * gw, gw), gw)
        group = lax.div(i, per_geometry)
        first = (group * rhs_count + r) * tile + lax.rem(i, per_geometry) * gw
        full = pl.ds(pl.multiple_of(first, gw), gw)
        bd, bw = col_features(table, ids_ref[:, full], len_ref[:, full], count_all)
        bd_buf[:, at] = bd
        bw_buf[:, at] = bw
        return carry

    lax.fori_loop(0, blk_count * per_geometry, col_geometry, 0)

    def far_step(group, n, rows):
        at = pl.ds(pl.multiple_of(n * nt, nt), nt)
        feats = pl.ds(pl.multiple_of(group * tile + n * nt, nt), nt)
        x = x_all[group, :, :, at].reshape(rhs_count * LANES, nt)
        out = far_tile(a_buf[rows, :], bd_buf[:, feats], bw_buf[:, feats], x)
        acc_re[rows, :] = acc_re[rows, :] + out[:mt]
        acc_im[rows, :] = acc_im[rows, :] + out[mt:]

    def own_tile(i, carry):
        rows = pl.ds(pl.multiple_of(lax.rem(i, chunks) * mt, mt), mt)
        far_step(b, lax.div(i, chunks), rows)
        return carry

    lax.fori_loop(0, per_tile * chunks, own_tile, 0)

    def forward(k, carry):
        gather_arrival(k).wait_recv()
        pass_on(k, mine).start()
        return carry

    lax.fori_loop(1, blk_count, forward, 0)

    def forwarded(k, carry):
        gather_copy(k).wait_send()
        pass_on(k, mine).wait_send()
        pass_on(k, theirs).wait_recv()
        return carry

    lax.fori_loop(1, blk_count, forwarded, 0)

    def y_copy(c, k, outbound):
        rows = pl.ds(pl.multiple_of(c * mt, mt), mt)
        other = lax.rem(r + k, rhs_count) if outbound else lax.rem(r - k + rhs_count, rhs_count)
        return pltpu.make_async_remote_copy(
            src_ref=y_send.at[other, rows],
            dst_ref=y_recv.at[r if outbound else other, rows],
            send_sem=y_ssem.at[c, k], recv_sem=y_rsem.at[c, k],
            device_id={"rhs": other}, device_id_type=MESH,
        )

    def row_chunk(c, carry):
        rows = pl.ds(pl.multiple_of(c * mt, mt), mt)

        def column(i, inner):
            group = lax.rem(b + 1 + lax.div(i, per_tile), blk_count)
            far_step(group, lax.rem(i, per_tile), rows)
            return inner

        lax.fori_loop(0, (blk_count - 1) * per_tile, column, 0)
        own = jnp.zeros((mt, LANES), F32)
        for q in range(rhs_count):
            lanes = slice(q * LANES, (q + 1) * LANES)
            y = combine(acc_re[rows, lanes], acc_im[rows, lanes], part_angles) + near_ref[q, rows, :]
            y_send[q, rows, :] = y.astype(BF16)
            own = own + jnp.where(r == q, y, 0.0)
        y_own[rows, :] = own

        def start(k, inner):
            y_copy(c, k, True).start()
            return inner

        lax.fori_loop(1, rhs_count, start, 0)
        return carry

    lax.fori_loop(0, chunks, row_chunk, 0)

    own_map = map_ref[:, pl.ds(pl.multiple_of(me * ROWS_DEV, ROWS_DEV), ROWS_DEV)]
    slots = send_slots(own_map, owners)
    place = lax.rem(own_map, jnp.int32(ROWS_DEV))
    sub_row = lax.broadcasted_iota(jnp.int32, (LANES, ROWS_DEV), 0)
    marks = jnp.where(
        sub_row == 2 * part_angles,
        place >> 6,
        jnp.where(sub_row == 2 * part_angles + 1, place & 63, 0),
    )
    total = y_own[...] + jnp.transpose(marks.astype(F32))

    for c in range(chunks):
        for k in range(1, rhs_count):
            y_copy(c, k, True).wait_send()
            y_copy(c, k, False).wait_recv()
    for k in range(1, rhs_count):
        total = total + y_recv[lax.rem(r - k + rhs_count, rhs_count)].astype(F32)
    flat = total.astype(BF16)

    def owner_copy(k, outbound):
        o = lax.rem(me + k, owners) if outbound else lax.rem(me - k + owners, owners)
        return pltpu.make_async_remote_copy(
            src_ref=go_buf.at[o],
            dst_ref=come_buf.at[me if outbound else o],
            send_sem=p_send.at[k], recv_sem=p_recv.at[k],
            device_id={"blk": lax.div(o, sub_count), "sub": lax.rem(o, sub_count)},
            device_id_type=MESH,
        )

    def outgoing(o):
        at = lax.broadcasted_iota(jnp.int32, (slot_rows, ROWS_DEV), 0) + o * slot_rows
        perm = jnp.where(at == slots, 1.0, 0.0).astype(BF16)
        return jnp.dot(perm, flat, preferred_element_type=F32).astype(BF16)

    def send_owner(k, carry):
        o = lax.rem(me + k, owners)
        go_buf[o] = outgoing(o)
        owner_copy(k, True).start()
        return carry

    lax.fori_loop(1, owners, send_owner, 0)
    come_buf[me] = outgoing(me)

    def owner_done(k, carry):
        owner_copy(k, True).wait_send()
        owner_copy(k, False).wait_recv()
        return carry

    lax.fori_loop(1, owners, owner_done, 0)

    arrived = come_buf[...].reshape(ROWS_DEV, LANES)
    turned = jnp.transpose(arrived.astype(F32))
    spot = turned[2 * part_angles : 2 * part_angles + 1] * 64.0 + turned[2 * part_angles + 1 : 2 * part_angles + 2]
    spot = spot.astype(jnp.int32)
    wide = 256

    def landing(i, carry):
        at = lax.broadcasted_iota(jnp.int32, (wide, ROWS_DEV), 0) + i * wide
        perm = jnp.where(at == spot, 1.0, 0.0).astype(BF16)
        moved = jnp.dot(perm, arrived, preferred_element_type=F32).astype(BF16)
        rows = []
        for q in range(wide // BS):
            value = dual_ref[i * (wide // BS) + q]
            piece = moved[q * BS : (q + 1) * BS]
            re = jnp.dot(value[:, :BS], piece, preferred_element_type=F32)
            im = jnp.dot(value[:, BS:], piece, preferred_element_type=F32)
            rows.append(combine(re, im, part_angles))
        result = jnp.transpose(jnp.concatenate(rows, 0))
        cols = pl.ds(pl.multiple_of(i * wide, wide), wide)
        out_ref[0, :, cols] = result[:part_angles]
        out_ref[1, :, cols] = result[part_angles : 2 * part_angles]
        return carry

    lax.fori_loop(0, ROWS_DEV // wide, landing, 0)


def body(currents, tri_cent, edge_tris, edge_len, near_col, near_val, refine_map, dual_blocks):
    blk_count = lax.axis_size("blk")
    rhs_count = lax.axis_size("rhs")
    sub_count = lax.axis_size("sub")
    angle_count, tile = currents.shape[1], currents.shape[2]
    part_angles = angle_count // rhs_count
    owners = blk_count * sub_count

    channels = 2 * part_angles
    cpad = -(-channels // 16) * 16
    near_sum, x_own = near_call(near_col, currents, near_val, rhs_count, cpad)
    wide = rhs_count * LANES
    chunks = ROWS_DEV // 512
    vmem = pl.BlockSpec(memory_space=pltpu.VMEM)
    dma = lambda *shape: pltpu.SemaphoreType.DMA(shape)
    return pl.pallas_call(
        functools.partial(whole_kernel, (blk_count, rhs_count, sub_count), part_angles),
        out_shape=jax.ShapeDtypeStruct((2, part_angles, ROWS_DEV), F32),
        in_specs=[vmem] * 7,
        out_specs=vmem,
        scratch_shapes=[
            pltpu.VMEM((ROWS_DEV, LANES), BF16),
            pltpu.VMEM((LANES, blk_count * tile), BF16),
            pltpu.VMEM((LANES, blk_count * tile), BF16),
            pltpu.VMEM((blk_count, rhs_count, LANES, tile), BF16),
            pltpu.VMEM((ROWS_DEV, wide), F32),
            pltpu.VMEM((ROWS_DEV, wide), F32),
            pltpu.VMEM((ROWS_DEV, LANES), F32),
            pltpu.VMEM((rhs_count, ROWS_DEV, LANES), BF16),
            pltpu.VMEM((rhs_count, ROWS_DEV, LANES), BF16),
            pltpu.VMEM((owners, ROWS_DEV // owners, LANES), BF16),
            pltpu.VMEM((owners, ROWS_DEV // owners, LANES), BF16),
            dma(blk_count), dma(blk_count), dma(blk_count), dma(blk_count),
            dma(chunks, rhs_count), dma(chunks, rhs_count), dma(owners), dma(owners),
            pltpu.VMEM((3 * (tri_cent.shape[1] // LANES), LANES), F32),
        ],
        compiler_params=pltpu.CompilerParams(
            collective_id=0, has_side_effects=True, vmem_limit_bytes=VMEM_LIMIT
        ),
    )(tri_cent, edge_tris, edge_len[None], x_own, near_sum, refine_map[None], dual_blocks)


def solution(mesh):
    in_specs = (
        P(None, None, ("parts", "blk", "rhs")),
        P(None, "parts"),
        P(None, "parts"),
        P("parts"),
        P(("parts", "blk", "sub"), "rhs"),
        P(("parts", "blk", "sub"), "rhs", None, None),
        P("parts"),
        P(("parts", "blk", "sub"), None, None),
    )
    out_specs = P(None, "rhs", ("parts", "blk", "sub"))
    return jax.shard_map(body, mesh=mesh, in_specs=in_specs, out_specs=out_specs, check_vma=False)
```

```python
import functools
import math

import jax
import jax.numpy as jnp
from jax import lax
from jax.experimental import pallas as pl
from jax.experimental.pallas import tpu as pltpu
from jax.sharding import PartitionSpec as P

ROWS_DEV = 1536
BS = 64
LANES = 128
CENTER = 5.0
SOFT2 = 0.1 * 0.1
SPAN2 = 9.0
CHARGE_TERM = 0.5
COS_C = (0.99995979, -19.73104169, 64.67343113, -82.40355036, 45.64655658)
SIN_C = (6.27863546, -41.09373103, 77.93035288, -56.0864031)
ROUNDER = 12582912.0

F32 = jnp.float32
BF16 = jnp.bfloat16
MESH = pl.DeviceIdType.MESH
NT = (((1,), (1,)), ((), ()))
VMEM_LIMIT = 56 * 1024 * 1024


def split3(x):
    h = x.astype(BF16).astype(F32)
    m = (x - h).astype(BF16).astype(F32)
    return h, m, (x - h - m).astype(BF16).astype(F32)


def lookup(table, ids):
    high = table.shape[0] // 3
    width = ids.shape[1]
    low_id = ids & (LANES - 1)
    high_id = ids >> 7
    lows = lax.broadcasted_iota(jnp.int32, (LANES, width), 0) == low_id
    onehot = jnp.where(lows, 1.0, 0.0).astype(BF16)
    picked = jnp.dot(
        table, jnp.concatenate([onehot] * 3, 0), preferred_element_type=F32
    )
    mask = lax.broadcasted_iota(jnp.int32, (high, width), 0) == high_id
    rows = [
        jnp.sum(jnp.where(mask, picked[c * high : (c + 1) * high], 0.0), axis=0, keepdims=True)
        for c in range(3)
    ]
    return jnp.concatenate(rows + [jnp.zeros((5, width), F32)], 0)


def make_table(tri):
    return jnp.concatenate([piece.astype(BF16) for piece in split3(tri)], 1)


def features(table, ids, lens, count_all, is_rows):
    width = ids.shape[1]
    plus, minus = lookup(table, ids[0:1]), lookup(table, ids[1:2])
    row = lax.broadcasted_iota(jnp.int32, (8, width), 0)
    pos = jnp.where(row < 3, 0.5 * (plus + minus) - CENTER, 0.0)
    norm = jnp.sum(pos * pos, axis=0, keepdims=True)
    ends = (minus - plus) * lens + jnp.where(row == 3, lens, 0.0)
    if is_rows:
        scale = 1.0
    else:
        norm = norm + SOFT2
        scale = jnp.where(row == 3, -CHARGE_TERM, 1.0 / SPAN2) / math.sqrt(count_all)
    ends = ends * scale
    h, m, l = split3(pos)
    nh, nm, nl = split3(norm)
    qh, ql, unused = split3(ends)
    norms = jnp.zeros((8, width), F32)
    first = 0 if is_rows else 3
    for k, piece in enumerate((nh, nm, nl)):
        norms = jnp.where(row == first + k, piece, norms)
    ones_at = (row >= 3) & (row < 6) if is_rows else row < 3
    norms = jnp.where(ones_at, 1.0, norms)
    if is_rows:
        h, m, l = -2.0 * h, -2.0 * m, -2.0 * l
        dist_rows = [h, h, m, h, l, m, norms]
        amp_rows = [qh, qh, ql]
    else:
        dist_rows = [h, m, h, l, h, m, norms]
        amp_rows = [qh, ql, qh]
    return dist_rows, amp_rows


def row_features(table, ids, lens, count_all):
    dist_rows, amp_rows = features(table, ids, lens, count_all, True)
    pad = jnp.zeros((48, ids.shape[1]), F32)
    return jnp.transpose(jnp.concatenate(dist_rows + amp_rows + [pad], 0)).astype(BF16)


def col_features(table, ids, lens, count_all):
    dist_rows, amp_rows = features(table, ids, lens, count_all, False)
    width = ids.shape[1]
    zeros = lambda rows: jnp.zeros((rows, width), F32)
    return (
        jnp.concatenate(dist_rows + [zeros(72)], 0).astype(BF16),
        jnp.concatenate([zeros(56)] + amp_rows + [zeros(48)], 0).astype(BF16),
    )


def tile_values(d2, weight):
    inv = lax.rsqrt(d2)
    dist = d2 * inv
    t = dist - ((dist + ROUNDER) - ROUNDER)
    u = t * t
    cosine = COS_C[4]
    for c in COS_C[3::-1]:
        cosine = cosine * u + c
    sine = SIN_C[3]
    for c in SIN_C[2::-1]:
        sine = sine * u + c
    amp = weight * inv
    return (amp * cosine).astype(BF16), ((amp * t) * sine).astype(BF16)


def far_tile(a, bd, bw, x):
    d2 = jnp.dot(a, bd, preferred_element_type=F32)
    weight = jnp.dot(a, bw, preferred_element_type=F32)
    kre, kim = tile_values(d2, weight)
    return lax.dot_general(jnp.concatenate([kre, kim], 0), x, NT, preferred_element_type=F32)


def combine(real_rows, imag_rows, part_angles):
    lane = lax.broadcasted_iota(jnp.int32, real_rows.shape, 1)
    ahead = pltpu.roll(imag_rows, LANES - part_angles, 1)
    behind = pltpu.roll(imag_rows, part_angles, 1)
    turned = jnp.where(lane < part_angles, -ahead, jnp.where(lane < 2 * part_angles, behind, 0.0))
    return real_rows + turned


def send_slots(own_map, owners):
    width = own_map.shape[1]
    slot_rows = width // owners
    target = lax.div(own_map, jnp.int32(ROWS_DEV))
    before = lax.broadcasted_iota(jnp.int32, (LANES, LANES), 0) < lax.broadcasted_iota(
        jnp.int32, (LANES, LANES), 1
    )
    triangle = jnp.where(before, 1.0, 0.0).astype(BF16)
    running = jnp.zeros((owners, 1), F32)
    ranks = []
    for k in range(width // LANES):
        part = target[:, k * LANES : (k + 1) * LANES]
        hits = lax.broadcasted_iota(jnp.int32, (owners, LANES), 0) == part
        onehot = jnp.where(hits, 1.0, 0.0)
        prior = running + jnp.dot(onehot.astype(BF16), triangle, preferred_element_type=F32)
        ranks.append(jnp.sum(onehot * prior, axis=0, keepdims=True))
        running = running + jnp.sum(onehot, axis=1, keepdims=True)
    return target * slot_rows + jnp.concatenate(ranks, 1).astype(jnp.int32)


def near_kernel(part_angles, col_ref, cur_ref, val_ref, y_ref, x_ref, x_pad, re_buf, im_buf):
    rhs_count, cpad, tile = x_ref.shape
    row_blocks, per_row = val_ref.shape[0], val_ref.shape[1]
    lane = lax.broadcasted_iota(jnp.int32, (BS, LANES), 1)
    pa = part_angles
    for q in range(rhs_count):
        pieces = [cur_ref[t, q * pa : (q + 1) * pa, :].astype(F32) for t in range(2)]
        pieces.append(jnp.zeros((LANES - 2 * pa, tile), F32))
        x_pad[q] = jnp.concatenate(pieces, 0).astype(BF16)
    x_ref[...] = x_pad[:, 0:cpad, :]

    def near_block(i, carry):
        total = jnp.zeros((2 * BS, rhs_count * LANES), F32)
        for j in range(per_row):
            local = lax.rem(col_ref[i, j], tile // BS)
            odd = lax.rem(local, 2)
            pair = lax.div(local, 2)
            value = val_ref[i, j].astype(F32)
            swapped = jnp.concatenate([value[:, BS:], value[:, :BS]], 1)
            keep = (lane >> 6) == odd
            re_lhs = jnp.where(keep, jnp.where(odd == 1, swapped, value), 0.0)
            im_lhs = jnp.where(keep, jnp.where(odd == 1, value, swapped), 0.0)
            lhs = jnp.concatenate([re_lhs, im_lhs], 0).astype(BF16)
            cols = x_pad[:, :, pl.ds(pl.multiple_of(pair * LANES, LANES), LANES)]
            cols = cols.reshape(rhs_count * LANES, LANES)
            total = total + lax.dot_general(lhs, cols, NT, preferred_element_type=F32)
        rows = pl.ds(pl.multiple_of(i * BS, BS), BS)
        re_buf[rows, :] = total[:BS]
        im_buf[rows, :] = total[BS:]
        return carry

    lax.fori_loop(0, row_blocks, near_block, 0, unroll=8)
    for q in range(rhs_count):
        lanes = slice(q * LANES, (q + 1) * LANES)
        y_ref[q] = combine(re_buf[:, lanes], im_buf[:, lanes], part_angles)


def near_call(near_col, currents, near_val, rhs_count, cpad):
    unused, angle_count, tile = currents.shape
    vmem = pl.BlockSpec(memory_space=pltpu.VMEM)
    return pl.pallas_call(
        functools.partial(near_kernel, angle_count // rhs_count),
        out_shape=[
            jax.ShapeDtypeStruct((rhs_count, ROWS_DEV, LANES), F32),
            jax.ShapeDtypeStruct((rhs_count, cpad, tile), BF16),
        ],
        in_specs=[pl.BlockSpec(memory_space=pltpu.SMEM), vmem, vmem],
        out_specs=[vmem, vmem],
        scratch_shapes=[
            pltpu.VMEM((rhs_count, LANES, tile), BF16),
            pltpu.VMEM((ROWS_DEV, rhs_count * LANES), F32),
            pltpu.VMEM((ROWS_DEV, rhs_count * LANES), F32),
        ],
        compiler_params=pltpu.CompilerParams(vmem_limit_bytes=VMEM_LIMIT),
    )(near_col, currents, near_val)


def whole_kernel(
    sizes, part_angles,
    tri_ref, ids_ref, len_ref, own_ref, near_ref, map_ref, dual_ref,
    out_ref,
    a_buf, bd_buf, bw_buf, x_all, acc_re, acc_im, y_own, y_send, y_recv, go_buf, come_buf,
    ag_send, ag_recv, fw_send, fw_recv, y_ssem, y_rsem, p_send, p_recv, tri_buf,
):
    blk_count, rhs_count, sub_count = sizes
    b, r, s = (lax.axis_index(name) for name in ("blk", "rhs", "sub"))
    cpad, tile = own_ref.shape[1], own_ref.shape[2]
    owners = blk_count * sub_count
    me = b * sub_count + s
    count_all = blk_count * rhs_count * tile
    half = rhs_count // sub_count
    slot_rows = ROWS_DEV // owners
    mt = 512
    chunks = ROWS_DEV // mt
    nt = tile
    per_tile = 1

    barrier = pltpu.get_barrier_semaphore()

    def greet_owner(k, carry):
        o = lax.rem(me + k, owners)
        pl.semaphore_signal(
            barrier, inc=1,
            device_id={"blk": lax.div(o, sub_count), "sub": lax.rem(o, sub_count)},
            device_id_type=MESH,
        )
        return carry

    def greet_rhs(k, carry):
        pl.semaphore_signal(
            barrier, inc=1, device_id={"rhs": lax.rem(r + k, rhs_count)}, device_id_type=MESH
        )
        return carry

    lax.fori_loop(1, owners, greet_owner, 0)
    lax.fori_loop(1, rhs_count, greet_rhs, 0)
    pl.semaphore_wait(barrier, owners - 1 + rhs_count - 1)

    mine = pl.ds(s * half, half)
    theirs = pl.ds((1 - s) * half, half)
    real = pl.ds(0, cpad)

    def gather_copy(k):
        return pltpu.make_async_remote_copy(
            src_ref=own_ref.at[mine],
            dst_ref=x_all.at[b, mine, real],
            send_sem=ag_send.at[k], recv_sem=ag_recv.at[k],
            device_id={"blk": lax.rem(b + k, blk_count)}, device_id_type=MESH,
        )

    def gather_arrival(k):
        source = lax.rem(b - k + blk_count, blk_count)
        return pltpu.make_async_remote_copy(
            src_ref=own_ref.at[mine],
            dst_ref=x_all.at[source, mine, real],
            send_sem=ag_send.at[k], recv_sem=ag_recv.at[k],
            device_id={"blk": source}, device_id_type=MESH,
        )

    def pass_on(k, which):
        source = lax.rem(b - k + blk_count, blk_count)
        return pltpu.make_async_remote_copy(
            src_ref=x_all.at[source, which, real],
            dst_ref=x_all.at[source, which, real],
            send_sem=fw_send.at[k], recv_sem=fw_recv.at[k],
            device_id={"sub": 1 - s}, device_id_type=MESH,
        )

    def start_gather(k, carry):
        gather_copy(k).start()
        return carry

    lax.fori_loop(1, blk_count, start_gather, 0)

    if cpad < LANES:
        x_all[:, :, cpad:, :] = jnp.zeros((blk_count, rhs_count, LANES - cpad, tile), BF16)
    x_all[b, :, 0:cpad, :] = own_ref[...]
    acc_re[...] = jnp.zeros_like(acc_re)
    acc_im[...] = jnp.zeros_like(acc_im)

    high = tri_ref.shape[1] // LANES
    for c in range(3):
        for h in range(high):
            tri_buf[c * high + h : c * high + h + 1, :] = tri_ref[c : c + 1, h * LANES : (h + 1) * LANES]
    table = make_table(tri_buf[...])
    gw = 512 if tile % 512 == 0 else LANES
    per_geometry = tile // gw

    def row_geometry(i, carry):
        at = pl.ds(pl.multiple_of(i * 512, 512), 512)
        full = pl.ds(pl.multiple_of(me * ROWS_DEV + i * 512, 512), 512)
        a_buf[at, :] = row_features(table, ids_ref[:, full], len_ref[:, full], count_all)
        return carry

    lax.fori_loop(0, ROWS_DEV // 512, row_geometry, 0, unroll=3)

    def col_geometry(i, carry):
        at = pl.ds(pl.multiple_of(i * gw, gw), gw)
        group = lax.div(i, per_geometry)
        first = (group * rhs_count + r) * tile + lax.rem(i, per_geometry) * gw
        full = pl.ds(pl.multiple_of(first, gw), gw)
        bd, bw = col_features(table, ids_ref[:, full], len_ref[:, full], count_all)
        bd_buf[:, at] = bd
        bw_buf[:, at] = bw
        return carry

    lax.fori_loop(0, blk_count * per_geometry, col_geometry, 0, unroll=2)

    def far_step(group, n, rows):
        at = pl.ds(pl.multiple_of(n * nt, nt), nt)
        feats = pl.ds(pl.multiple_of(group * tile + n * nt, nt), nt)
        x = x_all[group, :, :, at].reshape(rhs_count * LANES, nt)
        out = far_tile(a_buf[rows, :], bd_buf[:, feats], bw_buf[:, feats], x)
        acc_re[rows, :] = acc_re[rows, :] + out[:mt]
        acc_im[rows, :] = acc_im[rows, :] + out[mt:]

    def own_tile(i, carry):
        rows = pl.ds(pl.multiple_of(lax.rem(i, chunks) * mt, mt), mt)
        far_step(b, lax.div(i, chunks), rows)
        return carry

    lax.fori_loop(0, per_tile * chunks, own_tile, 0)

    def forward(k, carry):
        gather_arrival(k).wait_recv()
        pass_on(k, mine).start()
        return carry

    lax.fori_loop(1, blk_count, forward, 0)

    def forwarded(k, carry):
        gather_copy(k).wait_send()
        pass_on(k, mine).wait_send()
        pass_on(k, theirs).wait_recv()
        return carry

    lax.fori_loop(1, blk_count, forwarded, 0)

    def y_copy(c, k, outbound):
        rows = pl.ds(pl.multiple_of(c * mt, mt), mt)
        other = lax.rem(r + k, rhs_count) if outbound else lax.rem(r - k + rhs_count, rhs_count)
        return pltpu.make_async_remote_copy(
            src_ref=y_send.at[other, rows],
            dst_ref=y_recv.at[r if outbound else other, rows],
            send_sem=y_ssem.at[c, k], recv_sem=y_rsem.at[c, k],
            device_id={"rhs": other}, device_id_type=MESH,
        )

    def row_chunk(c, carry):
        rows = pl.ds(pl.multiple_of(c * mt, mt), mt)

        def column(i, inner):
            group = lax.rem(b + 1 + lax.div(i, per_tile), blk_count)
            far_step(group, lax.rem(i, per_tile), rows)
            return inner

        lax.fori_loop(0, (blk_count - 1) * per_tile, column, 0)
        own = jnp.zeros((mt, LANES), F32)
        for q in range(rhs_count):
            lanes = slice(q * LANES, (q + 1) * LANES)
            y = combine(acc_re[rows, lanes], acc_im[rows, lanes], part_angles) + near_ref[q, rows, :]
            y_send[q, rows, :] = y.astype(BF16)
            own = own + jnp.where(r == q, y, 0.0)
        y_own[rows, :] = own

        def start(k, inner):
            y_copy(c, k, True).start()
            return inner

        lax.fori_loop(1, rhs_count, start, 0)
        return carry

    lax.fori_loop(0, chunks, row_chunk, 0)

    own_map = map_ref[:, pl.ds(pl.multiple_of(me * ROWS_DEV, ROWS_DEV), ROWS_DEV)]
    slots = send_slots(own_map, owners)
    place = lax.rem(own_map, jnp.int32(ROWS_DEV))
    sub_row = lax.broadcasted_iota(jnp.int32, (LANES, ROWS_DEV), 0)
    marks = jnp.where(
        sub_row == 2 * part_angles,
        place >> 6,
        jnp.where(sub_row == 2 * part_angles + 1, place & 63, 0),
    )
    total = y_own[...] + jnp.transpose(marks.astype(F32))

    for c in range(chunks):
        for k in range(1, rhs_count):
            y_copy(c, k, True).wait_send()
            y_copy(c, k, False).wait_recv()
    for k in range(1, rhs_count):
        total = total + y_recv[lax.rem(r - k + rhs_count, rhs_count)].astype(F32)
    flat = total.astype(BF16)

    def owner_copy(k, outbound):
        o = lax.rem(me + k, owners) if outbound else lax.rem(me - k + owners, owners)
        return pltpu.make_async_remote_copy(
            src_ref=go_buf.at[o],
            dst_ref=come_buf.at[me if outbound else o],
            send_sem=p_send.at[k], recv_sem=p_recv.at[k],
            device_id={"blk": lax.div(o, sub_count), "sub": lax.rem(o, sub_count)},
            device_id_type=MESH,
        )

    def outgoing(o):
        at = lax.broadcasted_iota(jnp.int32, (slot_rows, ROWS_DEV), 0) + o * slot_rows
        perm = jnp.where(at == slots, 1.0, 0.0).astype(BF16)
        return jnp.dot(perm, flat, preferred_element_type=F32).astype(BF16)

    def send_owner(k, carry):
        o = lax.rem(me + k, owners)
        go_buf[o] = outgoing(o)
        owner_copy(k, True).start()
        return carry

    lax.fori_loop(1, owners, send_owner, 0)
    come_buf[me] = outgoing(me)

    def owner_done(k, carry):
        owner_copy(k, True).wait_send()
        owner_copy(k, False).wait_recv()
        return carry

    lax.fori_loop(1, owners, owner_done, 0)

    arrived = come_buf[...].reshape(ROWS_DEV, LANES)
    turned = jnp.transpose(arrived.astype(F32))
    spot = turned[2 * part_angles : 2 * part_angles + 1] * 64.0 + turned[2 * part_angles + 1 : 2 * part_angles + 2]
    spot = spot.astype(jnp.int32)
    wide = 256

    def landing(i, carry):
        at = lax.broadcasted_iota(jnp.int32, (wide, ROWS_DEV), 0) + i * wide
        perm = jnp.where(at == spot, 1.0, 0.0).astype(BF16)
        moved = jnp.dot(perm, arrived, preferred_element_type=F32).astype(BF16)
        rows = []
        for q in range(wide // BS):
            value = dual_ref[i * (wide // BS) + q]
            piece = moved[q * BS : (q + 1) * BS]
            re = jnp.dot(value[:, :BS], piece, preferred_element_type=F32)
            im = jnp.dot(value[:, BS:], piece, preferred_element_type=F32)
            rows.append(combine(re, im, part_angles))
        result = jnp.transpose(jnp.concatenate(rows, 0))
        cols = pl.ds(pl.multiple_of(i * wide, wide), wide)
        out_ref[0, :, cols] = result[:part_angles]
        out_ref[1, :, cols] = result[part_angles : 2 * part_angles]
        return carry

    lax.fori_loop(0, ROWS_DEV // wide, landing, 0, unroll=2)


def body(currents, tri_cent, edge_tris, edge_len, near_col, near_val, refine_map, dual_blocks):
    blk_count = lax.axis_size("blk")
    rhs_count = lax.axis_size("rhs")
    sub_count = lax.axis_size("sub")
    angle_count, tile = currents.shape[1], currents.shape[2]
    part_angles = angle_count // rhs_count
    owners = blk_count * sub_count

    channels = 2 * part_angles
    cpad = -(-channels // 16) * 16
    near_sum, x_own = near_call(near_col, currents, near_val, rhs_count, cpad)
    wide = rhs_count * LANES
    chunks = ROWS_DEV // 512
    vmem = pl.BlockSpec(memory_space=pltpu.VMEM)
    dma = lambda *shape: pltpu.SemaphoreType.DMA(shape)
    return pl.pallas_call(
        functools.partial(whole_kernel, (blk_count, rhs_count, sub_count), part_angles),
        out_shape=jax.ShapeDtypeStruct((2, part_angles, ROWS_DEV), F32),
        in_specs=[vmem] * 7,
        out_specs=vmem,
        scratch_shapes=[
            pltpu.VMEM((ROWS_DEV, LANES), BF16),
            pltpu.VMEM((LANES, blk_count * tile), BF16),
            pltpu.VMEM((LANES, blk_count * tile), BF16),
            pltpu.VMEM((blk_count, rhs_count, LANES, tile), BF16),
            pltpu.VMEM((ROWS_DEV, wide), F32),
            pltpu.VMEM((ROWS_DEV, wide), F32),
            pltpu.VMEM((ROWS_DEV, LANES), F32),
            pltpu.VMEM((rhs_count, ROWS_DEV, LANES), BF16),
            pltpu.VMEM((rhs_count, ROWS_DEV, LANES), BF16),
            pltpu.VMEM((owners, ROWS_DEV // owners, LANES), BF16),
            pltpu.VMEM((owners, ROWS_DEV // owners, LANES), BF16),
            dma(blk_count), dma(blk_count), dma(blk_count), dma(blk_count),
            dma(chunks, rhs_count), dma(chunks, rhs_count), dma(owners), dma(owners),
            pltpu.VMEM((3 * (tri_cent.shape[1] // LANES), LANES), F32),
        ],
        compiler_params=pltpu.CompilerParams(
            collective_id=0, has_side_effects=True, vmem_limit_bytes=VMEM_LIMIT
        ),
    )(tri_cent, edge_tris, edge_len[None], x_own, near_sum, refine_map[None], dual_blocks)


def solution(mesh):
    in_specs = (
        P(None, None, ("parts", "blk", "rhs")),
        P(None, "parts"),
        P(None, "parts"),
        P("parts"),
        P(("parts", "blk", "sub"), "rhs"),
        P(("parts", "blk", "sub"), "rhs", None, None),
        P("parts"),
        P(("parts", "blk", "sub"), None, None),
    )
    out_specs = P(None, "rhs", ("parts", "blk", "sub"))
    return jax.shard_map(body, mesh=mesh, in_specs=in_specs, out_specs=out_specs, check_vma=False)
```
